32 devices in a mesh: groups: 2 (over x), wide: 16 (over z, y, core).
Axes of the slice: x: 2, y: 2, z: 4, core: 2. Of those that a mesh axis runs over, the one named last changes fastest.
Arguments:
- hidden_states: bfloat16 [2048, 64, 1024], P(('groups', 'wide')), parts along dimension 0, may hold values from -6 to 6
- block_owner: int32 [2048, 1], P(('groups', 'wide')), parts along dimension 0, may hold values from 0 to 15; in each aligned block of 64 rows (0 to 63, 64 to 127, ...) at most 8 rows name the same one
- token_doc: int32 [2048, 64], P(('groups', 'wide')), parts along dimension 0, may hold values from 0 to 7, never falling along the last dimension, each value on 1 to 32 neighbouring positions
- token_live: int32 [2048, 64], P(('groups', 'wide')), parts along dimension 0, may hold values 0 or 1
- proj_weight: bfloat16 [1024, 128], replicated, may hold values from -0.1875 to 0.1875
- queries: bfloat16 [2048, 128], P(('groups', 'wide')), parts along dimension 0, may hold values from -1.5 to 1.5
Outputs:
- scores: float32 [256, 1024], P(('groups', 'wide')), parts along dimension 0
The draws below stay inside these ranges and needn't reach their ends.
There are 2 independent parts, one for each index of `groups`. The reference program is written for one: setup_inputs(seed, part) draws one part's arguments, and reference() takes and returns one part's arrays. A program takes and returns all parts, laid end to end along the dimension named above; an argument that names none is the same for every part. Nothing has to cross between parts.
Inputs may be any that keep to these rules, and one draw needn't show every extreme that they name: `block_owner`: among the 64 blocks of one index of wide no owner is named by more than 8 blocks, a bound that some block reaches. `token_doc`: within a block the ids never fall and every id appears.
All inputs are finite; a program needn't handle non-finite values. No bound on the sum of `token_live` on one device may be relied on, other than what follows from the above.
Results may differ from the reference program's by a relative error of at most 0.0011.
Values may be sent and summed in bfloat16 or wider, within the bound.
A program may use at most 64 MiB of HBM per device.

```python
import math
import jax
import jax.numpy as jnp
import numpy as np
from jax import lax

D = 1024
DIM = 128
BLOCK = 64
B_DEV = 64
DOC_DEV = 8
MOST = 8
BLOCKS = 1024
QUERIES = 1024
DOCS = 128
N_WIDE = 16


def place_ends(entries, stream_key, low, top_value):
    place = [jax.random.randint(jax.random.fold_in(stream_key, axis), (), 0, length) for axis, length in enumerate(entries.shape)]
    widest = entries.shape.index(max(entries.shape))
    next_to = place[:widest] + [(place[widest] + 1) % entries.shape[widest]] + place[widest + 1:]
    return entries.at[tuple(place)].set(low).at[tuple(next_to)].set(top_value)


def levels(own_key, extent, shards, low, top_value):
    factor_of, own = 1.0, jax.random.fold_in(own_key, 6)
    for dim, shards_of in shards:
        steps = jnp.exp(jax.random.uniform(jax.random.fold_in(own, dim), (shards_of,), jnp.float32, low / len(shards), top_value / len(shards)))
        factor_of = factor_of * jnp.repeat(steps, extent[dim] // shards_of).reshape([-1 if axis == dim else 1 for axis in range(len(extent))])
    return factor_of


def length_profile(number_of, total, most, skew):
    portions = [(1 << 20) // math.isqrt(rank ** skew) + 1 for rank in range(2, number_of + 1)]
    spare, counts = total - most - (number_of - 1), [1] * (number_of - 1)
    while spare > 0:
        movable = [i for i in range(number_of - 1) if counts[i] < most]
        mass, budget = sum([portions[i] for i in movable]), spare
        for i in movable:
            addition = min(most - counts[i], max(1, budget * portions[i] // mass), spare)
            counts[i] = counts[i] + addition
            spare = spare - addition
    return np.array([most] + counts)


def uneven_parts(rng, amount, total, limit, skew):
    if amount == 2:
        one = jax.random.randint(rng, (), max(1, total - limit), min(limit, total - 1) + 1)
        return jnp.stack([one, total - one])
    sizes = jnp.asarray(length_profile(amount, total, limit, skew), jnp.int32)
    pairs = (amount - 1) // 2
    donor, taker = sizes[1:1 + 2 * pairs:2], sizes[2:2 + 2 * pairs:2]
    margin = jnp.minimum(donor - 1, limit - taker)
    shifted = jax.random.randint(jax.random.fold_in(rng, 1), (pairs,), 0, 1 << 20) % (margin + 1)
    sizes = sizes.at[1:1 + 2 * pairs:2].set(donor - shifted).at[2:2 + 2 * pairs:2].set(taker + shifted)
    return sizes[jax.random.permutation(jax.random.fold_in(rng, 2), amount)]


def deal_out(stream_key, own, number, rows, amount, top, limit, skew):
    sequence = jax.random.permutation(stream_key, amount)
    packed, ordinary = shares(amount, rows * top, limit, skew, True), shares(amount, rows * top, limit, skew, False)
    places = jnp.arange(amount)

    def named(sizes, turn):
        used = int((sizes > 0).sum())
        fixed = max(1, used // 4)
        shifted = fixed + (places - fixed + turn * (used - fixed)) % max(1, amount - fixed)
        return jnp.zeros((amount,), jnp.int32).at[sequence[jnp.where(places < fixed, places, shifted)]].set(jnp.asarray(sizes, jnp.int32))

    sizes = jnp.where(number % 4 == 0, named(packed, number // 4), named(ordinary, number - number // 4 - 1))
    mixed = jax.random.permutation(jax.random.fold_in(own, 3), amount)
    source_of, receiver = mixed[0:amount // 2 * 2:2], mixed[1:amount // 2 * 2:2]
    margin = jnp.minimum(sizes[source_of] - 1, limit - sizes[receiver]) // 2
    margin = jnp.where((source_of == sequence[0]) | (receiver == sequence[0]) | (sizes[receiver] == 0), 0, jnp.maximum(margin, 0))
    shifted = jax.random.randint(jax.random.fold_in(own, 4), (amount // 2,), 0, 1 << 20) % (margin + 1)
    sizes = sizes.at[source_of].add(-shifted).at[receiver].add(shifted)
    items = jnp.searchsorted(jnp.cumsum(sizes), jnp.arange(rows * top), side="right").astype(jnp.int32)
    listing = items.reshape(top, rows).T
    listing = listing[jax.random.permutation(jax.random.fold_in(own, 1), rows)]
    turn = jax.random.randint(jax.random.fold_in(own, 2), (rows, 1), 0, top)
    return jnp.take_along_axis(listing, (jnp.arange(top)[None, :] + turn) % top, axis=1)


def shares(number_of, total, bound, skew, full):
    loads = [(1 << 20) // math.isqrt(grade ** skew) + 1 for grade in range(1, number_of + 1)]
    largest = bound if full else min(bound, max(-(-total // number_of), total * loads[0] // sum(loads)))
    least = 1 if total - largest >= number_of - 1 else 0
    given, surplus = [largest] + [least] * (number_of - 1), total - largest - least * (number_of - 1)
    while surplus > 0:
        candidates = [i for i in range(1, number_of) if given[i] < largest] or [i for i in range(1, number_of) if given[i] < bound]
        whole, budget = sum([loads[i] for i in candidates]), surplus
        for i in candidates:
            addition = min(bound - given[i], max(1, budget * loads[i] // whole), surplus)
            given[i] = given[i] + addition
            surplus = surplus - addition
    return np.array(given)


def scatter_about(own_key, dims, spread, most, pieces=(), dtype=jnp.bfloat16):
    result = spread * jax.random.normal(own_key, dims, jnp.float32)
    if pieces:
        result = result * levels(own_key, dims, pieces, -0.22, 0.18)
    return jnp.clip(result, -most, most).astype(dtype)


def setup_inputs(seed: int = 0, part: int = 0) -> dict:
    streams_of = jax.random.split(jax.random.key(seed), 7)
    part_keys = jax.random.split(jax.random.fold_in(streams_of[6], part), 7)
    hidden_states = scatter_about(part_keys[0], (BLOCKS, BLOCK, D), 1.0, 6.0, ((0, 16),))
    block_owner_keys = jax.random.split(jax.random.fold_in(part_keys[1], 1), BLOCKS // B_DEV)
    block_owner_turns = jax.random.permutation(jax.random.fold_in(part_keys[1], 3), BLOCKS // B_DEV)
    block_owner = jax.vmap(lambda own, number: deal_out(jax.random.fold_in(part_keys[1], 2), own, number, B_DEV, N_WIDE, 1, MOST, 2))(block_owner_keys, block_owner_turns).reshape((BLOCKS, 1))
    token_doc = jax.vmap(lambda own: jnp.searchsorted(jnp.cumsum(uneven_parts(own, DOC_DEV, BLOCK, BLOCK // 2, 2)), jnp.arange(BLOCK), side="right"))(jax.random.split(part_keys[2], BLOCKS)).reshape((BLOCKS, BLOCK)).astype(jnp.int32)
    token_live = place_ends((jax.random.randint(part_keys[3], (BLOCKS, BLOCK), 0, 8) < 7).astype(jnp.int32), jax.random.fold_in(part_keys[3], 1), 0, 1)
    proj_weight = scatter_about(streams_of[4], (D, DIM), D ** -0.5, 0.1875)
    queries = scatter_about(part_keys[5], (QUERIES, DIM), 0.25, 1.5, ((0, 16),))
    return {"hidden_states": hidden_states, "block_owner": block_owner, "token_doc": token_doc, "token_live": token_live, "proj_weight": proj_weight, "queries": queries}


def reference(hidden_states, block_owner, token_doc, token_live, proj_weight, queries):
    nblocks, block_len, model_width = hidden_states.shape
    projected = jnp.dot(hidden_states.reshape(nblocks * block_len, model_width), proj_weight, preferred_element_type=jnp.float32)
    vectors = projected * lax.rsqrt(lax.optimization_barrier(jnp.sum(projected * projected, axis=1, keepdims=True)) + 1e-06)
    vectors = vectors.astype(jnp.bfloat16).reshape(nblocks, block_len, -1)
    doc_code = jnp.where(token_live == 1, token_doc, -1).astype(jnp.int32)
    owners = block_owner[:, 0].astype(jnp.int32)
    query_count = queries.shape[0]

    def visit(table, group_item):
        block_vec, block_code, owner = group_item
        similar = lax.dot_general(queries.astype(jnp.float32), block_vec.astype(jnp.float32), (((1,), (1,)), ((), ())))
        partial_value = jnp.stack([lax.optimization_barrier(jnp.max(jnp.where(block_code[None, :] == doc_slot, similar, -1000000000.0), axis=1)) for doc_slot in range(DOC_DEV)])
        first_row = (owner * DOC_DEV).astype(jnp.int32)
        current = lax.dynamic_slice(table, (first_row, jnp.int32(0)), (DOC_DEV, query_count))
        table = lax.dynamic_update_slice(table, jnp.maximum(current, partial_value), (first_row, jnp.int32(0)))
        return (table, None)
    start_table = jnp.full((DOCS, query_count), -1000000000.0, jnp.float32)
    table, unused = lax.scan(visit, start_table, (vectors, doc_code, owners))
    return jnp.where(table > -100000000.0, table, jnp.float32(0.0))
```

```python
import functools

import jax
import jax.numpy as jnp
from jax import lax
from jax.experimental import pallas as pl
from jax.experimental.pallas import tpu as pltpu
from jax.sharding import PartitionSpec as P

DOC_DEV = 8
LOW = -1000000000.0
MESH = pl.DeviceIdType.MESH


def slot_table(owners, owner_count, capacity):
    nblocks = owners.shape[0]
    place = jnp.arange(nblocks, dtype=jnp.int32)
    same = (owners[:, None] == owners[None, :]) & (place[:, None] < place[None, :])
    rank = jnp.sum(same.astype(jnp.int32), axis=0)
    key = owners * capacity + rank
    matches = key[None, :] == jnp.arange(owner_count * capacity, dtype=jnp.int32)[:, None]
    return nblocks + jnp.sum(jnp.where(matches, place[None, :] - nblocks, 0), axis=1)


def kernel(
    n,
    capacity,
    chunk,
    piece,
    table,
    hidden,
    doc,
    live,
    weight,
    queries,
    out,
    hid,
    vec,
    codes,
    qall,
    partial,
    send,
    recv,
    hid_sem,
    qs_sem,
    qr_sem,
    s_sem,
    r_sem,
):
    nblocks, block = doc.shape
    dim = weight.shape[1]
    nq = queries.shape[0]
    tokens = nblocks * block
    pieces = tokens // piece
    chunks = (n * nq) // chunk
    me = lax.axis_index("wide")

    def stream(i):
        rows = pl.ds(pl.multiple_of(i * piece, piece), piece)
        return pltpu.make_async_copy(hidden.at[rows], hid.at[rows], hid_sem.at[i])

    @pl.loop(0, pieces)
    def _(i):
        stream(i).start()

    barrier = pltpu.get_barrier_semaphore()

    @pl.loop(1, n)
    def _(k):
        pl.semaphore_signal(
            barrier, inc=1, device_id={"wide": lax.rem(me + k, n)}, device_id_type=MESH
        )

    mine = pl.ds(pl.multiple_of(me * nq, nq), nq)

    code = jnp.where(live[...] == 1, doc[...], -1).astype(jnp.float32).astype(jnp.bfloat16)
    rows_of = lax.broadcasted_iota(jnp.int32, (nblocks, dim), 0)

    @pl.loop(0, nblocks)
    def _(b):
        pick = (rows_of == b).astype(jnp.float32).astype(jnp.bfloat16)
        codes[pl.ds(pl.multiple_of(b * block, block), block), :] = lax.dot_general(
            code, pick, (((0,), (0,)), ((), ())), preferred_element_type=jnp.float32
        )

    partial[nblocks] = jnp.full(partial.shape[1:], LOW, jnp.float32)
    qall[mine, :] = queries[...]
    pl.semaphore_wait(barrier, n - 1)

    def spread(k):
        return pltpu.make_async_remote_copy(
            src_ref=queries,
            dst_ref=qall.at[mine],
            send_sem=qs_sem.at[k],
            recv_sem=qr_sem.at[k],
            device_id={"wide": lax.rem(me + k, n)},
            device_id_type=MESH,
        )

    @pl.loop(1, n)
    def _(k):
        spread(k).start()

    @pl.loop(0, pieces)
    def _(i):
        stream(i).wait()
        rows = pl.ds(pl.multiple_of(i * piece, piece), piece)
        projected = jnp.dot(hid[rows, :], weight[...], preferred_element_type=jnp.float32)
        scale = lax.rsqrt(jnp.sum(projected * projected, axis=1, keepdims=True) + 1e-06)
        vec[rows, :] = (projected * scale).astype(jnp.bfloat16)

    @pl.loop(1, n)
    def _(k):
        spread(k).wait()

    group = 4 if nblocks % 4 == 0 else 1

    def ship(c, k):
        return pltpu.make_async_remote_copy(
            src_ref=send.at[c, k],
            dst_ref=recv.at[c, k],
            send_sem=s_sem.at[c, k],
            recv_sem=r_sem.at[c, k],
            device_id={"wide": lax.rem(me + k, n)},
            device_id_type=MESH,
        )

    @pl.loop(0, chunks)
    def _(c):
        asked = qall[pl.ds(pl.multiple_of(c * chunk, chunk), chunk), :]

        @pl.loop(0, nblocks // group)
        def _(g):
            rows = pl.ds(pl.multiple_of(g * group * block, group * block), group * block)
            similar = lax.dot_general(
                vec[rows, :], asked, (((1,), (1,)), ((), ())), preferred_element_type=jnp.float32
            )
            named = codes[rows, :]
            for b in range(group):
                part = similar[b * block : (b + 1) * block]
                which = named[b * block : (b + 1) * block]
                which = jnp.concatenate([which] * (chunk // dim), axis=1)
                for d in range(DOC_DEV):
                    kept = jnp.where(which == float(d), part, LOW)
                    partial[g * group + b, d] = jnp.max(
                        kept.reshape(block // 8, 8, chunk), axis=0
                    )

        @pl.loop(0, n)
        def _(k):
            owner = lax.rem(me + k, n)
            best = partial[table[owner * capacity]]
            for s in range(1, capacity):
                best = jnp.maximum(best, partial[table[owner * capacity + s]])
            send[c, k] = jnp.max(best, axis=1)

        @pl.loop(1, n)
        def _(k):
            ship(c, k).start()

    @pl.loop(0, chunks)
    def _(c):
        def take(k, best):
            ship(c, k).wait()
            return jnp.maximum(best, recv[c, k])

        best = lax.fori_loop(1, n, take, send[c, 0])
        out[:, pl.ds(pl.multiple_of(c * chunk, chunk), chunk)] = jnp.where(
            best > -100000000.0, best, 0.0
        )


def local(hidden_states, block_owner, token_doc, token_live, proj_weight, queries):
    nblocks, block, width = hidden_states.shape
    n = lax.axis_size("wide")
    capacity = max(2, (2 * nblocks + n - 1) // n)
    tokens = nblocks * block
    dim = proj_weight.shape[1]
    nq = queries.shape[0]
    total = n * nq
    chunk = min(256, total)
    chunks = total // chunk
    piece = min(512, tokens)
    table = slot_table(block_owner[:, 0], n, capacity)
    vmem = pl.BlockSpec(memory_space=pltpu.VMEM)
    return pl.pallas_call(
        functools.partial(kernel, n, capacity, chunk, piece),
        out_shape=jax.ShapeDtypeStruct((DOC_DEV, total), jnp.float32),
        in_specs=[
            pl.BlockSpec(memory_space=pltpu.SMEM),
            pl.BlockSpec(memory_space=pl.ANY),
            vmem,
            vmem,
            vmem,
            vmem,
        ],
        out_specs=vmem,
        scratch_shapes=[
            pltpu.VMEM((tokens, width), jnp.bfloat16),
            pltpu.VMEM((tokens, dim), jnp.bfloat16),
            pltpu.VMEM((tokens, dim), jnp.float32),
            pltpu.VMEM((total, dim), jnp.bfloat16),
            pltpu.VMEM((nblocks + 1, DOC_DEV, 8, chunk), jnp.float32),
            pltpu.VMEM((chunks, n, DOC_DEV, chunk), jnp.float32),
            pltpu.VMEM((chunks, n, DOC_DEV, chunk), jnp.float32),
            pltpu.SemaphoreType.DMA((tokens // piece,)),
            pltpu.SemaphoreType.DMA((n,)),
            pltpu.SemaphoreType.DMA((n,)),
            pltpu.SemaphoreType.DMA((chunks, n)),
            pltpu.SemaphoreType.DMA((chunks, n)),
        ],
        compiler_params=pltpu.CompilerParams(
            collective_id=0, has_side_effects=True, vmem_limit_bytes=50 * 1024 * 1024
        ),
    )(
        table,
        hidden_states.reshape(tokens, width),
        token_doc,
        token_live,
        proj_weight,
        queries,
    )


def solution(mesh):
    placed = (
        P(("groups", "wide"), None, None),
        P(("groups", "wide"), None),
        P(("groups", "wide"), None),
        P(("groups", "wide"), None),
        P(),
        P(("groups", "wide"), None),
    )
    return jax.shard_map(
        local, mesh=mesh, in_specs=placed, out_specs=P(("groups", "wide"), None), check_vma=False
    )
```

```python
import functools

import jax
import jax.numpy as jnp
from jax import lax
from jax.experimental import pallas as pl
from jax.experimental.pallas import tpu as pltpu
from jax.sharding import PartitionSpec as P

DOC_DEV = 8
MOST_TOKENS = 32
LOW = -1000000000.0
MESH = pl.DeviceIdType.MESH


def slot_table(owners, owner_count, capacity):
    nblocks = owners.shape[0]
    slots = owner_count * capacity
    down = lax.broadcasted_iota(jnp.int32, (nblocks, nblocks), 0)
    along = lax.broadcasted_iota(jnp.int32, (nblocks, nblocks), 1)
    own = jnp.broadcast_to(owners, (nblocks, nblocks))
    across = jnp.sum(jnp.where(down == along, own, 0), axis=0, keepdims=True)
    earlier = jnp.where((own == across) & (along < down), 1, 0)
    rank = jnp.sum(earlier, axis=1, keepdims=True)
    key = owners * capacity + rank
    slot = lax.broadcasted_iota(jnp.int32, (nblocks, slots), 1)
    block = lax.broadcasted_iota(jnp.int32, (nblocks, slots), 0)
    held = jnp.where(slot == key, block - nblocks, 0)
    return nblocks + jnp.sum(held, axis=0, keepdims=True)


def kernel(
    n,
    capacity,
    chunk,
    piece,
    hidden,
    owner_hbm,
    doc_hbm,
    live_hbm,
    weight_hbm,
    queries_hbm,
    out,
    owners,
    doc,
    live,
    weight,
    queries,
    tablev,
    table,
    hid,
    vec,
    codes,
    qall,
    partial,
    send,
    recv,
    in_sem,
    hid_sem,
    qs_sem,
    qr_sem,
    s_sem,
    r_sem,
):
    nblocks, block = doc.shape
    dim = weight.shape[1]
    nq = queries.shape[0]
    tokens = nblocks * block
    pieces = tokens // piece
    chunks = (n * nq) // chunk
    me = lax.axis_index("wide")

    def stream(i):
        rows = pl.ds(pl.multiple_of(i * piece, piece), piece)
        return pltpu.make_async_copy(hidden.at[rows], hid.at[rows], hid_sem.at[i])

    small = [
        pltpu.make_async_copy(src, dst, in_sem.at[i])
        for i, (src, dst) in enumerate(
            (
                (queries_hbm, queries),
                (owner_hbm, owners),
                (doc_hbm, doc),
                (live_hbm, live),
                (weight_hbm, weight),
            )
        )
    ]
    for copy in small:
        copy.start()

    @pl.loop(0, pieces)
    def _(i):
        stream(i).start()

    barrier = pltpu.get_barrier_semaphore()

    @pl.loop(1, n)
    def _(k):
        pl.semaphore_signal(
            barrier, inc=1, device_id={"wide": lax.rem(me + k, n)}, device_id_type=MESH
        )

    mine = pl.ds(pl.multiple_of(me * nq, nq), nq)

    small[0].wait()
    qall[mine, :] = queries[...]
    pl.semaphore_wait(barrier, n - 1)

    def spread(k):
        return pltpu.make_async_remote_copy(
            src_ref=queries,
            dst_ref=qall.at[mine],
            send_sem=qs_sem.at[k],
            recv_sem=qr_sem.at[k],
            device_id={"wide": lax.rem(me + k, n)},
            device_id_type=MESH,
        )

    @pl.loop(1, n)
    def _(k):
        spread(k).start()

    small[1].wait()
    tablev[...] = slot_table(owners[...], n, capacity)
    to_scalars = pltpu.make_async_copy(tablev, table, in_sem.at[5])
    to_scalars.start()
    partial[nblocks] = jnp.full(partial.shape[1:], LOW, jnp.float32)

    small[2].wait()
    small[3].wait()
    code = jnp.where(live[...] == 1, doc[...], -1).astype(jnp.float32).astype(jnp.bfloat16)
    unit = lax.broadcasted_iota(jnp.int32, (nblocks, dim), 0) == lax.broadcasted_iota(
        jnp.int32, (nblocks, dim), 1
    )
    turned = lax.dot_general(
        code,
        unit.astype(jnp.float32).astype(jnp.bfloat16),
        (((0,), (0,)), ((), ())),
        preferred_element_type=jnp.float32,
    )
    for b in range(nblocks):
        codes[b * block : (b + 1) * block, :] = jnp.broadcast_to(turned[:, b : b + 1], (block, dim))
    small[4].wait()

    @pl.loop(0, pieces)
    def _(i):
        stream(i).wait()
        rows = pl.ds(pl.multiple_of(i * piece, piece), piece)
        projected = jnp.dot(hid[rows, :], weight[...], preferred_element_type=jnp.float32)
        scale = lax.rsqrt(jnp.sum(projected * projected, axis=1, keepdims=True) + 1e-06)
        vec[rows, :] = (projected * scale).astype(jnp.bfloat16)

    to_scalars.wait()

    @pl.loop(1, n)
    def _(k):
        spread(k).wait()

    group = 8 if nblocks % 8 == 0 else 1

    def ship(c, k):
        return pltpu.make_async_remote_copy(
            src_ref=send.at[c, k],
            dst_ref=recv.at[c, k],
            send_sem=s_sem.at[c, k],
            recv_sem=r_sem.at[c, k],
            device_id={"wide": lax.rem(me + k, n)},
            device_id_type=MESH,
        )

    @pl.loop(0, chunks)
    def _(c):
        asked = qall[pl.ds(pl.multiple_of(c * chunk, chunk), chunk), :]

        @pl.loop(0, nblocks // group)
        def _(g):
            rows = pl.ds(pl.multiple_of(g * group * block, group * block), group * block)
            similar = lax.dot_general(
                vec[rows, :], asked, (((1,), (1,)), ((), ())), preferred_element_type=jnp.float32
            )
            named = codes[rows, :]
            for b in range(group):
                part = similar[b * block : (b + 1) * block]
                which = named[b * block : (b + 1) * block]
                for d in range(DOC_DEV):
                    first = max(d, block - MOST_TOKENS * (DOC_DEV - d)) // 8 * 8
                    last = -(-min(MOST_TOKENS * (d + 1), block - (DOC_DEV - 1 - d)) // 8) * 8
                    keep = which[first:last] == float(d)
                    for h in range(0, chunk, dim):
                        kept = jnp.where(keep, part[first:last, h : h + dim], LOW)
                        partial[g * group + b, d, :, h : h + dim] = jnp.max(
                            kept.reshape((last - first) // 8, 8, dim), axis=0
                        )

        @pl.loop(0, n)
        def _(k):
            owner = lax.rem(me + k, n)
            best = None
            for s in range(capacity):
                at = jnp.clip(table[0, owner * capacity + s], 0, nblocks)
                best = partial[at] if best is None else jnp.maximum(best, partial[at])
            send[c, k] = jnp.max(best, axis=1)

        @pl.loop(1, n)
        def _(k):
            ship(c, k).start()

    @pl.loop(0, chunks)
    def _(c):
        def take(k, best):
            ship(c, k).wait()
            return jnp.maximum(best, recv[c, k])

        best = lax.fori_loop(1, n, take, send[c, 0])
        out[:, pl.ds(pl.multiple_of(c * chunk, chunk), chunk)] = jnp.where(
            best > -100000000.0, best, 0.0
        )


def local(hidden_states, block_owner, token_doc, token_live, proj_weight, queries):
    nblocks, block, width = hidden_states.shape
    n = lax.axis_size("wide")
    capacity = max(2, (2 * nblocks + n - 1) // n)
    tokens = nblocks * block
    dim = proj_weight.shape[1]
    nq = queries.shape[0]
    total = n * nq
    chunk = min(512, total)
    chunks = total // chunk
    piece = min(512, tokens)
    vmem = pl.BlockSpec(memory_space=pltpu.VMEM)
    return pl.pallas_call(
        functools.partial(kernel, n, capacity, chunk, piece),
        out_shape=jax.ShapeDtypeStruct((DOC_DEV, total), jnp.float32),
        in_specs=[pl.BlockSpec(memory_space=pl.ANY)] * 6,
        out_specs=vmem,
        scratch_shapes=[
            pltpu.VMEM(block_owner.shape, jnp.int32),
            pltpu.VMEM(token_doc.shape, jnp.int32),
            pltpu.VMEM(token_live.shape, jnp.int32),
            pltpu.VMEM(proj_weight.shape, jnp.bfloat16),
            pltpu.VMEM(queries.shape, jnp.bfloat16),
            pltpu.VMEM((1, n * capacity), jnp.int32),
            pltpu.SMEM((1, n * capacity), jnp.int32),
            pltpu.VMEM((tokens, width), jnp.bfloat16),
            pltpu.VMEM((tokens, dim), jnp.bfloat16),
            pltpu.VMEM((tokens, dim), jnp.float32),
            pltpu.VMEM((total, dim), jnp.bfloat16),
            pltpu.VMEM((nblocks + 1, DOC_DEV, 8, chunk), jnp.float32),
            pltpu.VMEM((chunks, n, DOC_DEV, chunk), jnp.float32),
            pltpu.VMEM((chunks, n, DOC_DEV, chunk), jnp.float32),
            pltpu.SemaphoreType.DMA((6,)),
            pltpu.SemaphoreType.DMA((tokens // piece,)),
            pltpu.SemaphoreType.DMA((n,)),
            pltpu.SemaphoreType.DMA((n,)),
            pltpu.SemaphoreType.DMA((chunks, n)),
            pltpu.SemaphoreType.DMA((chunks, n)),
        ],
        compiler_params=pltpu.CompilerParams(
            collective_id=0, has_side_effects=True, vmem_limit_bytes=50 * 1024 * 1024
        ),
    )(
        hidden_states.reshape(tokens, width),
        block_owner,
        token_doc,
        token_live,
        proj_weight,
        queries,
    )


def solution(mesh):
    placed = (
        P(("groups", "wide"), None, None),
        P(("groups", "wide"), None),
        P(("groups", "wide"), None),
        P(("groups", "wide"), None),
        P(),
        P(("groups", "wide"), None),
    )
    return jax.shard_map(
        local, mesh=mesh, in_specs=placed, out_specs=P(("groups", "wide"), None), check_vma=False
    )
```

```python
import functools

import jax
import jax.numpy as jnp
from jax import lax
from jax.experimental import pallas as pl
from jax.experimental.pallas import tpu as pltpu
from jax.sharding import PartitionSpec as P

DOC_DEV = 8
MOST_TOKENS = 32
LOW = -1000000000.0
MESH = pl.DeviceIdType.MESH


def slot_table(owners, owner_count, capacity):
    nblocks = owners.shape[0]
    slots = owner_count * capacity
    down = lax.broadcasted_iota(jnp.int32, (nblocks, nblocks), 0)
    along = lax.broadcasted_iota(jnp.int32, (nblocks, nblocks), 1)
    own = jnp.broadcast_to(owners, (nblocks, nblocks))
    across = jnp.sum(jnp.where(down == along, own, 0), axis=0, keepdims=True)
    earlier = jnp.where((own == across) & (along < down), 1, 0)
    rank = jnp.sum(earlier, axis=1, keepdims=True)
    key = owners * capacity + rank
    slot = lax.broadcasted_iota(jnp.int32, (nblocks, slots), 1)
    block = lax.broadcasted_iota(jnp.int32, (nblocks, slots), 0)
    held = jnp.where(slot == key, block - nblocks, 0)
    return nblocks + jnp.sum(held, axis=0, keepdims=True)


def kernel(
    n,
    capacity,
    chunk,
    piece,
    hidden,
    owner_hbm,
    doc_hbm,
    live_hbm,
    weight_hbm,
    queries_hbm,
    out,
    owners,
    doc,
    live,
    weight,
    queries,
    tablev,
    table,
    hid,
    vec,
    codes,
    qall,
    partial,
    send,
    recv,
    in_sem,
    hid_sem,
    qs_sem,
    qr_sem,
    s_sem,
    r_sem,
):
    nblocks, block = doc.shape
    dim = weight.shape[1]
    nq = queries.shape[0]
    tokens = nblocks * block
    pieces = tokens // piece
    chunks = (n * nq) // chunk
    me = lax.axis_index("wide")

    def stream(i):
        rows = pl.ds(pl.multiple_of(i * piece, piece), piece)
        return pltpu.make_async_copy(hidden.at[rows], hid.at[rows], hid_sem.at[i])

    small = [
        pltpu.make_async_copy(src, dst, in_sem.at[i])
        for i, (src, dst) in enumerate(
            (
                (queries_hbm, queries),
                (owner_hbm, owners),
                (doc_hbm, doc),
                (live_hbm, live),
                (weight_hbm, weight),
            )
        )
    ]
    for copy in small:
        copy.start()

    @pl.loop(0, pieces)
    def _(i):
        stream(i).start()

    barrier = pltpu.get_barrier_semaphore()

    @pl.loop(1, n)
    def _(k):
        pl.semaphore_signal(
            barrier, inc=1, device_id={"wide": lax.rem(me + k, n)}, device_id_type=MESH
        )

    mine = pl.ds(pl.multiple_of(me * nq, nq), nq)

    small[0].wait()
    qall[mine, :] = queries[...]
    pl.semaphore_wait(barrier, n - 1)

    def spread(k):
        return pltpu.make_async_remote_copy(
            src_ref=queries,
            dst_ref=qall.at[mine],
            send_sem=qs_sem.at[k],
            recv_sem=qr_sem.at[k],
            device_id={"wide": lax.rem(me + k, n)},
            device_id_type=MESH,
        )

    @pl.loop(1, n)
    def _(k):
        spread(k).start()

    small[1].wait()
    tablev[...] = slot_table(owners[...], n, capacity)
    to_scalars = pltpu.make_async_copy(tablev, table, in_sem.at[5])
    to_scalars.start()
    partial[nblocks] = jnp.full(partial.shape[1:], LOW, jnp.float32)

    small[2].wait()
    small[3].wait()
    code = jnp.where(live[...] == 1, doc[...], -1).astype(jnp.float32).astype(jnp.bfloat16)
    unit = lax.broadcasted_iota(jnp.int32, (nblocks, dim), 0) == lax.broadcasted_iota(
        jnp.int32, (nblocks, dim), 1
    )
    turned = lax.dot_general(
        code,
        unit.astype(jnp.float32).astype(jnp.bfloat16),
        (((0,), (0,)), ((), ())),
        preferred_element_type=jnp.float32,
    )
    for b in range(nblocks):
        codes[b * block : (b + 1) * block, :] = jnp.broadcast_to(turned[:, b : b + 1], (block, dim))
    small[4].wait()

    @pl.loop(0, pieces)
    def _(i):
        stream(i).wait()
        rows = pl.ds(pl.multiple_of(i * piece, piece), piece)
        projected = jnp.dot(hid[rows, :], weight[...], preferred_element_type=jnp.float32)
        scale = lax.rsqrt(jnp.sum(projected * projected, axis=1, keepdims=True) + 1e-06)
        vec[rows, :] = (projected * scale).astype(jnp.bfloat16)

    to_scalars.wait()

    @pl.loop(1, n)
    def _(k):
        spread(k).wait()

    group = 16 if nblocks % 16 == 0 else 1

    def ship(c, k):
        return pltpu.make_async_remote_copy(
            src_ref=send.at[c, k],
            dst_ref=recv.at[c, k],
            send_sem=s_sem.at[c, k],
            recv_sem=r_sem.at[c, k],
            device_id={"wide": lax.rem(me + k, n)},
            device_id_type=MESH,
        )

    @pl.loop(0, chunks)
    def _(c):
        asked = qall[pl.ds(pl.multiple_of(c * chunk, chunk), chunk), :]

        @pl.loop(0, nblocks // group)
        def _(g):
            rows = pl.ds(pl.multiple_of(g * group * block, group * block), group * block)
            similar = lax.dot_general(
                vec[rows, :], asked, (((1,), (1,)), ((), ())), preferred_element_type=jnp.float32
            )
            named = codes[rows, :]
            for b in range(group):
                part = similar[b * block : (b + 1) * block]
                which = named[b * block : (b + 1) * block]
                for d in range(DOC_DEV):
                    first = max(d, block - MOST_TOKENS * (DOC_DEV - d)) // 8 * 8
                    last = -(-min(MOST_TOKENS * (d + 1), block - (DOC_DEV - 1 - d)) // 8) * 8
                    keep = which[first:last] == float(d)
                    for h in range(0, chunk, dim):
                        kept = jnp.where(keep, part[first:last, h : h + dim], LOW)
                        partial[g * group + b, d, :, h : h + dim] = jnp.max(
                            kept.reshape((last - first) // 8, 8, dim), axis=0
                        )

        @pl.loop(0, n)
        def _(k):
            owner = lax.rem(me + k, n)
            best = None
            for s in range(capacity):
                at = jnp.clip(table[0, owner * capacity + s], 0, nblocks)
                best = partial[at] if best is None else jnp.maximum(best, partial[at])
            send[c, k] = jnp.max(best, axis=1)

            @pl.when(k > 0)
            def _():
                ship(c, k).start()

    @pl.loop(0, chunks)
    def _(c):
        def take(k, best):
            ship(c, k).wait()
            return jnp.maximum(best, recv[c, k])

        best = lax.fori_loop(1, n, take, send[c, 0])
        out[:, pl.ds(pl.multiple_of(c * chunk, chunk), chunk)] = jnp.where(
            best > -100000000.0, best, 0.0
        )


def local(hidden_states, block_owner, token_doc, token_live, proj_weight, queries):
    nblocks, block, width = hidden_states.shape
    n = lax.axis_size("wide")
    capacity = max(2, (2 * nblocks + n - 1) // n)
    tokens = nblocks * block
    dim = proj_weight.shape[1]
    nq = queries.shape[0]
    total = n * nq
    chunk = min(512, total)
    chunks = total // chunk
    piece = min(512, tokens)
    vmem = pl.BlockSpec(memory_space=pltpu.VMEM)
    return pl.pallas_call(
        functools.partial(kernel, n, capacity, chunk, piece),
        out_shape=jax.ShapeDtypeStruct((DOC_DEV, total), jnp.float32),
        in_specs=[pl.BlockSpec(memory_space=pl.ANY)] * 6,
        out_specs=vmem,
        scratch_shapes=[
            pltpu.VMEM(block_owner.shape, jnp.int32),
            pltpu.VMEM(token_doc.shape, jnp.int32),
            pltpu.VMEM(token_live.shape, jnp.int32),
            pltpu.VMEM(proj_weight.shape, jnp.bfloat16),
            pltpu.VMEM(queries.shape, jnp.bfloat16),
            pltpu.VMEM((1, n * capacity), jnp.int32),
            pltpu.SMEM((1, n * capacity), jnp.int32),
            pltpu.VMEM((tokens, width), jnp.bfloat16),
            pltpu.VMEM((tokens, dim), jnp.bfloat16),
            pltpu.VMEM((tokens, dim), jnp.float32),
            pltpu.VMEM((total, dim), jnp.bfloat16),
            pltpu.VMEM((nblocks + 1, DOC_DEV, 8, chunk), jnp.float32),
            pltpu.VMEM((chunks, n, DOC_DEV, chunk), jnp.float32),
            pltpu.VMEM((chunks, n, DOC_DEV, chunk), jnp.float32),
            pltpu.SemaphoreType.DMA((6,)),
            pltpu.SemaphoreType.DMA((tokens // piece,)),
            pltpu.SemaphoreType.DMA((n,)),
            pltpu.SemaphoreType.DMA((n,)),
            pltpu.SemaphoreType.DMA((chunks, n)),
            pltpu.SemaphoreType.DMA((chunks, n)),
        ],
        compiler_params=pltpu.CompilerParams(
            collective_id=0, has_side_effects=True, vmem_limit_bytes=50 * 1024 * 1024
        ),
    )(
        hidden_states.reshape(tokens, width),
        block_owner,
        token_doc,
        token_live,
        proj_weight,
        queries,
    )


def solution(mesh):
    placed = (
        P(("groups", "wide"), None, None),
        P(("groups", "wide"), None),
        P(("groups", "wide"), None),
        P(("groups", "wide"), None),
        P(),
        P(("groups", "wide"), None),
    )
    return jax.shard_map(
        local, mesh=mesh, in_specs=placed, out_specs=P(("groups", "wide"), None), check_vma=False
    )
```

```python
import functools

import jax
import jax.numpy as jnp
from jax import lax
from jax.experimental import pallas as pl
from jax.experimental.pallas import tpu as pltpu
from jax.sharding import PartitionSpec as P

DOC_DEV = 8
MOST_TOKENS = 32
LOW = -1000000000.0
MESH = pl.DeviceIdType.MESH


def slot_table(owners, owner_count, capacity):
    nblocks = owners.shape[0]
    slots = owner_count * capacity
    down = lax.broadcasted_iota(jnp.int32, (nblocks, nblocks), 0)
    along = lax.broadcasted_iota(jnp.int32, (nblocks, nblocks), 1)
    own = jnp.broadcast_to(owners, (nblocks, nblocks))
    across = jnp.sum(jnp.where(down == along, own, 0), axis=0, keepdims=True)
    earlier = jnp.where((own == across) & (along < down), 1, 0)
    rank = jnp.sum(earlier, axis=1, keepdims=True)
    key = owners * capacity + rank
    slot = lax.broadcasted_iota(jnp.int32, (nblocks, slots), 1)
    block = lax.broadcasted_iota(jnp.int32, (nblocks, slots), 0)
    held = jnp.where(slot == key, block - nblocks, 0)
    return nblocks + jnp.sum(held, axis=0, keepdims=True)


def kernel(
    n,
    capacity,
    chunk,
    piece,
    hidden,
    owner_hbm,
    doc_hbm,
    live_hbm,
    weight_hbm,
    queries_hbm,
    out,
    owners,
    doc,
    live,
    weight,
    queries,
    tablev,
    table,
    hid,
    vec,
    codes,
    qall,
    partial,
    send,
    recv,
    in_sem,
    hid_sem,
    qs_sem,
    qr_sem,
    s_sem,
    r_sem,
):
    nblocks, block = doc.shape
    dim = weight.shape[1]
    nq = queries.shape[0]
    tokens = nblocks * block
    pieces = tokens // piece
    chunks = (n * nq) // chunk
    me = lax.axis_index("wide")

    def stream(i):
        rows = pl.ds(pl.multiple_of(i * piece, piece), piece)
        return pltpu.make_async_copy(hidden.at[rows], hid.at[rows], hid_sem.at[i])

    small = [
        pltpu.make_async_copy(src, dst, in_sem.at[i])
        for i, (src, dst) in enumerate(
            (
                (queries_hbm, queries),
                (owner_hbm, owners),
                (doc_hbm, doc),
                (live_hbm, live),
                (weight_hbm, weight),
            )
        )
    ]
    for copy in small:
        copy.start()

    @pl.loop(0, pieces)
    def _(i):
        stream(i).start()

    barrier = pltpu.get_barrier_semaphore()

    @pl.loop(1, n)
    def _(k):
        pl.semaphore_signal(
            barrier, inc=1, device_id={"wide": lax.rem(me + k, n)}, device_id_type=MESH
        )

    mine = pl.ds(pl.multiple_of(me * nq, nq), nq)

    small[0].wait()
    qall[mine, :] = queries[...]
    pl.semaphore_wait(barrier, n - 1)

    def spread(k):
        return pltpu.make_async_remote_copy(
            src_ref=queries,
            dst_ref=qall.at[mine],
            send_sem=qs_sem.at[k],
            recv_sem=qr_sem.at[k],
            device_id={"wide": lax.rem(me + k, n)},
            device_id_type=MESH,
        )

    @pl.loop(1, n)
    def _(k):
        spread(k).start()

    small[1].wait()
    tablev[...] = slot_table(owners[...], n, capacity)
    to_scalars = pltpu.make_async_copy(tablev, table, in_sem.at[5])
    to_scalars.start()
    partial[nblocks] = jnp.full(partial.shape[1:], LOW, jnp.float32)

    small[2].wait()
    small[3].wait()
    code = jnp.where(live[...] == 1, doc[...], -1).astype(jnp.float32).astype(jnp.bfloat16)
    unit = lax.broadcasted_iota(jnp.int32, (nblocks, dim), 0) == lax.broadcasted_iota(
        jnp.int32, (nblocks, dim), 1
    )
    turned = lax.dot_general(
        code,
        unit.astype(jnp.float32).astype(jnp.bfloat16),
        (((0,), (0,)), ((), ())),
        preferred_element_type=jnp.float32,
    )
    for b in range(nblocks):
        codes[b * block : (b + 1) * block, :] = jnp.broadcast_to(turned[:, b : b + 1], (block, dim))
    small[4].wait()

    @pl.loop(0, pieces)
    def _(i):
        stream(i).wait()
        rows = pl.ds(pl.multiple_of(i * piece, piece), piece)
        projected = jnp.dot(hid[rows, :], weight[...], preferred_element_type=jnp.float32)
        scale = lax.rsqrt(jnp.sum(projected * projected, axis=1, keepdims=True) + 1e-06)
        vec[rows, :] = (projected * scale).astype(jnp.bfloat16)

    to_scalars.wait()

    @pl.loop(1, n)
    def _(k):
        spread(k).wait()

    group = 32 if nblocks % 32 == 0 else 1

    def ship(c, k):
        return pltpu.make_async_remote_copy(
            src_ref=send.at[c, k],
            dst_ref=recv.at[c, k],
            send_sem=s_sem.at[c, k],
            recv_sem=r_sem.at[c, k],
            device_id={"wide": lax.rem(me + k, n)},
            device_id_type=MESH,
        )

    @pl.loop(0, chunks)
    def _(c):
        asked = qall[pl.ds(pl.multiple_of(c * chunk, chunk), chunk), :]

        @pl.loop(0, nblocks // group)
        def _(g):
            rows = pl.ds(pl.multiple_of(g * group * block, group * block), group * block)
            similar = lax.dot_general(
                vec[rows, :], asked, (((1,), (1,)), ((), ())), preferred_element_type=jnp.float32
            )
            named = codes[rows, :]
            for b in range(group):
                part = similar[b * block : (b + 1) * block]
                which = named[b * block : (b + 1) * block]
                for d in range(DOC_DEV):
                    first = max(d, block - MOST_TOKENS * (DOC_DEV - d)) // 8 * 8
                    last = -(-min(MOST_TOKENS * (d + 1), block - (DOC_DEV - 1 - d)) // 8) * 8
                    keep = which[first:last] == float(d)
                    for h in range(0, chunk, dim):
                        kept = jnp.where(keep, part[first:last, h : h + dim], LOW)
                        partial[g * group + b, d, :, h : h + dim] = jnp.max(
                            kept.reshape((last - first) // 8, 8, dim), axis=0
                        )

        @pl.loop(0, n)
        def _(k):
            owner = lax.rem(me + k, n)
            best = None
            for s in range(capacity):
                at = jnp.clip(table[0, owner * capacity + s], 0, nblocks)
                best = partial[at] if best is None else jnp.maximum(best, partial[at])
            send[c, k] = jnp.max(best, axis=1)

            @pl.when(k > 0)
            def _():
                ship(c, k).start()

    @pl.loop(0, chunks)
    def _(c):
        def take(k, best):
            ship(c, k).wait()
            return jnp.maximum(best, recv[c, k])

        best = lax.fori_loop(1, n, take, send[c, 0])
        out[:, pl.ds(pl.multiple_of(c * chunk, chunk), chunk)] = jnp.where(
            best > -100000000.0, best, 0.0
        )


def local(hidden_states, block_owner, token_doc, token_live, proj_weight, queries):
    nblocks, block, width = hidden_states.shape
    n = lax.axis_size("wide")
    capacity = max(2, (2 * nblocks + n - 1) // n)
    tokens = nblocks * block
    dim = proj_weight.shape[1]
    nq = queries.shape[0]
    total = n * nq
    chunk = min(512, total)
    chunks = total // chunk
    piece = min(512, tokens)
    vmem = pl.BlockSpec(memory_space=pltpu.VMEM)
    return pl.pallas_call(
        functools.partial(kernel, n, capacity, chunk, piece),
        out_shape=jax.ShapeDtypeStruct((DOC_DEV, total), jnp.float32),
        in_specs=[pl.BlockSpec(memory_space=pl.ANY)] * 6,
        out_specs=vmem,
        scratch_shapes=[
            pltpu.VMEM(block_owner.shape, jnp.int32),
            pltpu.VMEM(token_doc.shape, jnp.int32),
            pltpu.VMEM(token_live.shape, jnp.int32),
            pltpu.VMEM(proj_weight.shape, jnp.bfloat16),
            pltpu.VMEM(queries.shape, jnp.bfloat16),
            pltpu.VMEM((1, n * capacity), jnp.int32),
            pltpu.SMEM((1, n * capacity), jnp.int32),
            pltpu.VMEM((tokens, width), jnp.bfloat16),
            pltpu.VMEM((tokens, dim), jnp.bfloat16),
            pltpu.VMEM((tokens, dim), jnp.float32),
            pltpu.VMEM((total, dim), jnp.bfloat16),
            pltpu.VMEM((nblocks + 1, DOC_DEV, 8, chunk), jnp.float32),
            pltpu.VMEM((chunks, n, DOC_DEV, chunk), jnp.float32),
            pltpu.VMEM((chunks, n, DOC_DEV, chunk), jnp.float32),
            pltpu.SemaphoreType.DMA((6,)),
            pltpu.SemaphoreType.DMA((tokens // piece,)),
            pltpu.SemaphoreType.DMA((n,)),
            pltpu.SemaphoreType.DMA((n,)),
            pltpu.SemaphoreType.DMA((chunks, n)),
            pltpu.SemaphoreType.DMA((chunks, n)),
        ],
        compiler_params=pltpu.CompilerParams(
            collective_id=0, has_side_effects=True, vmem_limit_bytes=50 * 1024 * 1024
        ),
    )(
        hidden_states.reshape(tokens, width),
        block_owner,
        token_doc,
        token_live,
        proj_weight,
        queries,
    )


def solution(mesh):
    placed = (
        P(("groups", "wide"), None, None),
        P(("groups", "wide"), None),
        P(("groups", "wide"), None),
        P(("groups", "wide"), None),
        P(),
        P(("groups", "wide"), None),
    )
    return jax.shard_map(
        local, mesh=mesh, in_specs=placed, out_specs=P(("groups", "wide"), None), check_vma=False
    )
```
